768 devices in a mesh: row: 8 (over z_hi, core), col: 96 (over x, y, z_lo).
Axes of the slice: x: 4, y: 8, z: 12 (z_hi: 4, z_lo: 3; z = z_hi * 3 + z_lo), core: 2. Of those that a mesh axis runs over, the one named last changes fastest.
Arguments:
- features: bfloat16 [98304, 128], P(('row', 'col')), may hold values from -6 to 6
- adj_blocks: bfloat16 [36864, 128, 128], P(('row', 'col')), as said below
- positions: int32 [768, 48], P(('row', 'col')), may hold values from 0 to 767, as said below
- counts: int32 [768], P(('row', 'col')), may hold values from 1 to 48, as said below
- w_in: bfloat16 [128, 256], replicated, may hold values from -0.5 to 0.5
- w_out: bfloat16 [256, 128], replicated, may hold values from -0.375 to 0.375
- cotangent: bfloat16 [98304, 128], P(('row', 'col')), may hold values from -0.01953125 to 0.01953125
Outputs:
- output: bfloat16 [98304, 128], P(('row', 'col'))
- grad_in: float32 [128, 256], replicated
- grad_out: float32 [256, 128], replicated
The draws below stay inside these ranges and needn't reach their ends.
Inputs may be any that keep to these rules, and one draw needn't show every extreme that they name: Each device's 48 positions are distinct tile positions; position p names output block p // 96 and input block p % 96. `counts`: the number of live slots of each device, counted from slot 0; later slots hold data that is not part of the adjacency. `adj_blocks`: entries are zero or positive; the share of nonzero entries differs from block to block.
All inputs are finite; a program needn't handle non-finite values.
Results may differ from the reference program's by a relative error of at most 0.003.
The reference program's roundings to bfloat16 on the way count: a program that leaves them out, or rounds other values in their place, can miss the bound.
Values may be sent and summed in bfloat16 or wider, within the bound.
No kernel may reach another device: no remote copies, remote signals or barrier semaphores. Data moves between devices by JAX's collectives and lax.ppermute only.
A program may use at most 64 MiB of HBM per device.

```python
import math
import jax
import jax.numpy as jnp
from jax import lax

F_IN = 128
HID = 256
CLASSES = 128
BLOCK = 128
ND = 128
KSLOT = 48
RB_T = 8
CB_T = 96
KMAX = 48
NODES = 98304
N_ROW = 8
N_COL = 96


def draw_positions(key, part):
    key = jax.random.fold_in(key, 11)
    capacity = RB_T * CB_T
    scores = jax.random.randint(key, (N_ROW * N_COL, capacity), 0, 1 << 20) * capacity
    scores = scores + jnp.arange(capacity)[None, :]
    order = jnp.argsort(scores, axis=1)
    return order[:, :KMAX].astype(jnp.int32)


def draw_counts(key, part):
    key = jax.random.fold_in(key, 12)
    first_key, second_key, third_key = jax.random.split(key, 3)
    total = N_ROW * N_COL
    first_factor = jax.random.randint(first_key, (total,), 0, KMAX)
    second_factor = jax.random.randint(second_key, (total,), 0, KMAX)
    values = 1 + first_factor * second_factor // KMAX
    fullest = jax.random.randint(third_key, (), 0, total)
    values = jnp.where(jnp.arange(total) == fullest, KMAX, values)
    return values.astype(jnp.int32)


def draw_adj_blocks(key, part):
    key = jax.random.fold_in(key, 13)
    density_key, mask_key, value_key = jax.random.split(key, 3)
    total = N_ROW * N_COL * KMAX
    shape = (total, BLOCK, BLOCK)
    density = jnp.exp(jax.random.uniform(density_key, (total, 1, 1), jnp.float32, math.log(0.05), math.log(0.6)))
    values = jax.random.uniform(value_key, shape, jnp.float32, 0.5, 1.5)
    scale = 2.5
    keep = jax.random.uniform(mask_key, shape, jnp.float32) < density
    spread_scale = scale * (BLOCK * KSLOT) ** (-0.5)
    return jnp.where(keep, spread_scale * values, 0.0).astype(jnp.bfloat16)


def block_levels(own_key, extent, pieces, smallest, high):
    level, own = 1.0, jax.random.fold_in(own_key, 6)
    for dim, parts in pieces:
        heights = jnp.exp(jax.random.uniform(jax.random.fold_in(own, dim), (parts,), jnp.float32, smallest / len(pieces), high / len(pieces)))
        level = level * jnp.repeat(heights, extent[dim] // parts).reshape([-1 if axis == dim else 1 for axis in range(len(extent))])
    return level


def normal_values(stream_key, dims, scale, limit, shards=(), held_as=jnp.bfloat16):
    values = jax.random.normal(stream_key, dims, jnp.float32) * scale
    if len(shards) > 0:
        values = block_levels(stream_key, dims, shards, -0.22, 0.18) * values
    return jnp.clip(values, min=-limit, max=limit).astype(held_as)


def setup_inputs(seed: int = 0) -> dict:
    key_of = jax.random.split(jax.random.key(seed), 8)
    return {
        "features": normal_values(key_of[0], (NODES, F_IN), 1.0, 6.0, ((0, 768),)),
        "adj_blocks": draw_adj_blocks(jax.random.fold_in(key_of[7], 71), 0),
        "positions": draw_positions(jax.random.fold_in(key_of[7], 71), 0),
        "counts": draw_counts(jax.random.fold_in(key_of[7], 71), 0),
        "w_in": normal_values(key_of[4], (F_IN, HID), F_IN ** -0.5, 0.5),
        "w_out": normal_values(key_of[5], (HID, CLASSES), HID ** -0.5, 0.375),
        "cotangent": normal_values(key_of[6], (NODES, CLASSES), (NODES ** -0.5), 0.01953125, ((0, 768),)),
    }


def expand_slots(places, count):
    slot_count = places.shape[0]
    live_mask = (jnp.arange(slot_count) < count).astype(jnp.float32)
    out_index = places // CB_T
    in_index = places % CB_T
    out_table = (out_index[:, None] == jnp.arange(RB_T)[None, :]).astype(jnp.float32) * live_mask[:, None]
    in_table = (in_index[:, None] == jnp.arange(CB_T)[None, :]).astype(jnp.float32) * live_mask[:, None]
    return out_index, in_index, out_table, in_table


def tile_forward(tile_blocks, places, count, group_rows):
    out_index, in_index, out_table, in_table = expand_slots(places, count)
    picked = group_rows[in_index].astype(jnp.float32)
    products = jnp.einsum("kij,kjf->kif", tile_blocks.astype(jnp.float32), picked, precision=lax.Precision.HIGHEST)
    return jnp.einsum("kr,kif->rif", out_table, products, precision=lax.Precision.HIGHEST)


def tile_backward(tile_blocks, places, count, group_rows):
    out_index, in_index, out_table, in_table = expand_slots(places, count)
    picked = group_rows[out_index].astype(jnp.float32)
    products = jnp.einsum("kji,kjf->kif", tile_blocks.astype(jnp.float32), picked, precision=lax.Precision.HIGHEST)
    return jnp.einsum("kc,kif->cif", in_table, products, precision=lax.Precision.HIGHEST)


def reference(features, adj_blocks, positions, counts, w_in, w_out, cotangent):
    grid_blocks = adj_blocks.reshape(N_ROW, N_COL, KMAX, BLOCK, BLOCK)
    grid_places = positions.reshape(N_ROW, N_COL, KMAX)
    grid_counts = counts.reshape(N_ROW, N_COL)

    def aggregate(values):
        width = values.shape[1]
        groups = values.reshape(N_ROW, CB_T, BLOCK, width)

        def over_rows(total, row_args):
            row_blocks, row_places, row_counts, group_rows = row_args

            def one_tile(tile_args):
                return tile_forward(tile_args[0], tile_args[1], tile_args[2], group_rows)

            return total + lax.map(one_tile, (row_blocks, row_places, row_counts)), None

        start = jnp.zeros((N_COL, RB_T, BLOCK, width), jnp.float32)
        total, unused = lax.scan(over_rows, start, (grid_blocks, grid_places, grid_counts, groups))
        return total.reshape(N_COL, N_ROW, ND, width).transpose(1, 0, 2, 3).reshape(NODES, width)

    def transpose_apply(values):
        width = values.shape[1]
        groups = values.reshape(N_ROW, N_COL, ND, width).transpose(1, 0, 2, 3).reshape(N_COL, RB_T, BLOCK, width)

        def one_row(row_args):
            row_blocks, row_places, row_counts = row_args

            def over_cols(total, col_args):
                tile_blocks, places, count, group_rows = col_args
                return total + tile_backward(tile_blocks, places, count, group_rows), None

            start = jnp.zeros((CB_T, BLOCK, width), jnp.float32)
            total, unused = lax.scan(over_cols, start, (row_blocks, row_places, row_counts, groups))
            return total

        return lax.map(one_row, (grid_blocks, grid_places, grid_counts)).reshape(NODES, width)

    s_one = aggregate(features).astype(jnp.bfloat16)
    hidden = jax.nn.relu(jnp.dot(s_one, w_in, preferred_element_type=jnp.float32)).astype(jnp.bfloat16)
    class_rows = jnp.dot(hidden, w_out, preferred_element_type=jnp.float32).astype(jnp.bfloat16)
    output = aggregate(class_rows).astype(jnp.bfloat16)
    d_two = transpose_apply(cotangent).astype(jnp.bfloat16)
    grad_out = jnp.dot(hidden.T, d_two, preferred_element_type=jnp.float32)
    d_hidden = jnp.dot(d_two, w_out.T, preferred_element_type=jnp.float32)
    masked = jnp.where(hidden > 0, d_hidden, 0.0).astype(jnp.bfloat16)
    grad_in = jnp.dot(s_one.T, masked, preferred_element_type=jnp.float32)
    return output, grad_in, grad_out
```

```python
import jax
import jax.numpy as jnp
from jax import lax
from jax.experimental import pallas as pl
from jax.experimental.pallas import tpu as pltpu
from jax.sharding import Mesh
from jax.sharding import PartitionSpec as P

SPLIT = {"zh": 4, "core": 2, "x": 4, "y": 8, "zl": 3}
ROW = ("zh", "core")
COL = ("x", "y", "zl")
ALL = ROW + COL
VMEM_LIMIT = 40 * 1024 * 1024


def forward_kernel(count_ref, place_ref, blocks_ref, rows_ref, sums_ref):
    in_blocks = rows_ref.shape[0]
    sums_ref[...] = jnp.zeros_like(sums_ref)

    def step(slot, carry):
        place = place_ref[0, slot]
        out_block = place // in_blocks
        in_block = place - out_block * in_blocks
        sums_ref[out_block] += jnp.dot(
            blocks_ref[slot], rows_ref[in_block], preferred_element_type=jnp.float32
        )
        return carry

    lax.fori_loop(0, count_ref[0], step, 0)


def backward_kernel(count_ref, place_ref, blocks_ref, rows_ref, sums_ref):
    in_blocks = sums_ref.shape[0]
    sums_ref[...] = jnp.zeros_like(sums_ref)

    def step(slot, carry):
        place = place_ref[0, slot]
        out_block = place // in_blocks
        in_block = place - out_block * in_blocks
        sums_ref[in_block] += lax.dot_general(
            blocks_ref[slot],
            rows_ref[out_block],
            (((0,), (0,)), ((), ())),
            preferred_element_type=jnp.float32,
        )
        return carry

    lax.fori_loop(0, count_ref[0], step, 0)


def tile_product(kernel, counts, positions, adj_blocks, rows, out_blocks, name):
    slots, size, width = adj_blocks.shape[0], adj_blocks.shape[1], rows.shape[2]
    smem = pl.BlockSpec(memory_space=pltpu.SMEM)
    vmem = pl.BlockSpec(memory_space=pltpu.VMEM)
    return pl.pallas_call(
        kernel,
        out_shape=jax.ShapeDtypeStruct((out_blocks, size, width), jnp.float32),
        in_specs=[smem, smem, vmem, vmem],
        out_specs=vmem,
        compiler_params=pltpu.CompilerParams(vmem_limit_bytes=VMEM_LIMIT),
        cost_estimate=pl.CostEstimate(
            flops=2 * slots * size * size * width,
            bytes_accessed=adj_blocks.nbytes + rows.nbytes + 4 * out_blocks * size * width,
            transcendentals=0,
        ),
        name=name,
    )(counts, positions, adj_blocks, rows)


def exchange(values, axes):
    return lax.all_to_all(values, axes, 0, 0)


def collect(node_rows):
    part = lax.all_gather(node_rows, "zl", axis=0)
    part = lax.all_gather(part, "y", axis=0)
    copies = jnp.broadcast_to(part[None], (lax.axis_size("x"),) + part.shape)
    whole = exchange(lax.optimization_barrier(copies), "x")
    return whole.reshape((-1,) + node_rows.shape)


def reduce_rows(partial_value):
    return jnp.sum(exchange(partial_value, ROW), axis=0)


def reduce_cols(partial_value):
    total = partial_value
    for axis in COL:
        size = lax.axis_size(axis)
        total = total.reshape((size, total.shape[0] // size) + total.shape[1:])
        total = jnp.sum(exchange(total, axis), axis=0)
    return total[0]


def sum_everywhere(values):
    width = values.shape[1]
    total = values.reshape(2, -1, width)
    total = jnp.sum(exchange(total, "core"), axis=0)
    planes = lax.axis_size("x") * lax.axis_size("y")
    total = total.reshape(planes, -1, width)
    total = jnp.sum(exchange(total, ("x", "y")), axis=0)
    total = jnp.sum(lax.all_gather(total, ("zh", "zl"), axis=0), axis=0)
    copies = jnp.broadcast_to(total[None], (planes,) + total.shape)
    total = exchange(lax.optimization_barrier(copies), ("x", "y")).reshape(-1, width)
    return lax.all_gather(total, "core", axis=0, tiled=True)


def local(features, adj_blocks, positions, counts, w_in, w_out, cotangent):
    block_size = adj_blocks.shape[1]
    nodes_dev = features.shape[0]
    out_blocks = lax.axis_size(ROW) * nodes_dev // block_size
    in_blocks = lax.axis_size(COL) * nodes_dev // block_size

    def forward(rows, name):
        return tile_product(
            forward_kernel, counts, positions, adj_blocks, rows, out_blocks, name
        )

    group_grad = lax.all_gather(cotangent, ROW, axis=0)
    partial_two = tile_product(
        backward_kernel, counts, positions, adj_blocks, group_grad, in_blocks, "backward"
    )
    d_two = reduce_cols(partial_two).astype(jnp.bfloat16)

    s_one = reduce_rows(forward(collect(features), "forward_one")).astype(jnp.bfloat16)
    hidden = jnp.maximum(jnp.dot(s_one, w_in, preferred_element_type=jnp.float32), 0.0).astype(
        jnp.bfloat16
    )
    class_rows = jnp.dot(hidden, w_out, preferred_element_type=jnp.float32).astype(jnp.bfloat16)
    output = reduce_rows(forward(collect(class_rows), "forward_two")).astype(jnp.bfloat16)

    local_out = jnp.einsum("nh,nc->hc", hidden, d_two, preferred_element_type=jnp.float32)
    d_hidden = jnp.einsum("nc,hc->nh", d_two, w_out, preferred_element_type=jnp.float32)
    masked = jnp.where(hidden > 0, d_hidden, 0.0).astype(jnp.bfloat16)
    local_in = jnp.einsum("nf,nh->fh", s_one, masked, preferred_element_type=jnp.float32)
    width = local_out.shape[1]
    halves = local_in.shape[1] // width
    parts = [local_in[:, i * width : (i + 1) * width] for i in range(halves)]
    grads = sum_everywhere(jnp.concatenate(parts + [local_out], axis=0))
    rows_in = local_in.shape[0]
    grad_in = jnp.concatenate(
        [grads[i * rows_in : (i + 1) * rows_in] for i in range(halves)], axis=1
    )
    grad_out = grads[halves * rows_in :]
    return (output, grad_in, grad_out)


def build(mesh, split):
    cut = Mesh(mesh.devices.reshape(tuple(split.values())), tuple(split))
    placed = (
        P(ALL, None),
        P(ALL, None, None),
        P(ALL, None),
        P(ALL),
        P(),
        P(),
        P(ALL, None),
    )
    return jax.shard_map(
        local,
        mesh=cut,
        in_specs=placed,
        out_specs=(P(ALL, None), P(), P()),
        check_vma=False,
    )


def solution(mesh):
    return build(mesh, SPLIT)
```

```python
import functools

import jax
import jax.numpy as jnp
from jax import lax
from jax.experimental import pallas as pl
from jax.experimental.pallas import tpu as pltpu
from jax.sharding import Mesh
from jax.sharding import PartitionSpec as P

SPLIT = {"zh": 4, "core": 2, "x": 4, "y": 8, "zl": 3}
ROW = ("zh", "core")
COL = ("x", "y", "zl")
ALL = ROW + COL
VMEM_LIMIT = 40 * 1024 * 1024


def ahead_of(place, here, size):
    return lax.rem(place - here + size, size)


def forward_kernel(spans, count_ref, place_ref, here_ref, blocks_ref, *refs):
    rows_refs, sums_ref = refs[:-1], refs[-1]
    per_group = rows_refs[0].shape[0]
    in_blocks = per_group * len(rows_refs)
    sums_ref[...] = jnp.zeros_like(sums_ref)

    def step(slot, carry):
        place = place_ref[0, slot]
        out_block = place // in_blocks
        in_block = place - out_block * in_blocks
        plane = in_block // per_group
        at = in_block - plane * per_group
        back_x = ahead_of(here_ref[0], plane, spans[0])
        for distance, rows_ref in enumerate(rows_refs):

            @pl.when(back_x == distance)
            def add(rows_ref=rows_ref):
                sums_ref[out_block] += jnp.dot(
                    blocks_ref[slot], rows_ref[at], preferred_element_type=jnp.float32
                )

        return carry

    lax.fori_loop(0, count_ref[0], step, 0)


def backward_kernel(spans, count_ref, place_ref, here_ref, blocks_ref, rows_ref, *refs):
    sums_refs, top_ref = refs[:-1], refs[-1]
    in_blocks = spans[0] * spans[1] * spans[2]
    for sums_ref in sums_refs:
        sums_ref[...] = jnp.zeros_like(sums_ref)

    def step(slot, top):
        place = place_ref[0, slot]
        out_block = place // in_blocks
        in_block = place - out_block * in_blocks
        line = in_block // spans[2]
        plane = line // spans[1]
        ahead_x = ahead_of(plane, here_ref[0], spans[0])
        at = in_block - plane * spans[1] * spans[2]
        block = blocks_ref[slot]
        product = lax.dot_general(
            block,
            rows_ref[out_block],
            (((0,), (0,)), ((), ())),
            preferred_element_type=jnp.float32,
        )
        for distance, sums_ref in enumerate(sums_refs):

            @pl.when(ahead_x == distance)
            def add(sums_ref=sums_ref):
                sums_ref[at] += product

        wide = block.astype(jnp.float32).reshape(-1, top.shape[0], top.shape[1])
        return jnp.maximum(top, jnp.max(wide, axis=0))

    top_ref[...] = lax.fori_loop(
        0, count_ref[0], step, jnp.zeros(top_ref.shape, jnp.float32)
    )


def after_kernel(values_ref, earlier_ref, out_ref):
    out_ref[...] = values_ref[...]


def after(values, earlier):
    return pl.pallas_call(
        after_kernel,
        out_shape=jax.ShapeDtypeStruct(values.shape, values.dtype),
        in_specs=[pl.BlockSpec(memory_space=pltpu.VMEM), pl.BlockSpec(memory_space=pl.ANY)],
        out_specs=pl.BlockSpec(memory_space=pltpu.VMEM),
        cost_estimate=pl.CostEstimate(flops=1, bytes_accessed=1, transcendentals=0),
        name="after",
    )(values, earlier)


def tile_product(kernel, counts, positions, here, adj_blocks, rows, outs, name, earlier=()):
    smem = pl.BlockSpec(memory_space=pltpu.SMEM)
    vmem = pl.BlockSpec(memory_space=pltpu.VMEM)
    outs = [jax.ShapeDtypeStruct(shape, jnp.float32) for shape in outs]
    waits = list(earlier)

    def body(count_ref, place_ref, here_ref, *refs):
        kernel(count_ref, place_ref, here_ref, *refs[len(waits) :])

    return pl.pallas_call(
        body,
        out_shape=outs,
        in_specs=[smem] * 3
        + [pl.BlockSpec(memory_space=pl.ANY)] * len(waits)
        + [vmem] * (1 + len(rows)),
        out_specs=[vmem] * len(outs),
        compiler_params=pltpu.CompilerParams(vmem_limit_bytes=VMEM_LIMIT),
        cost_estimate=pl.CostEstimate(flops=1, bytes_accessed=1, transcendentals=0),
        name=name,
    )(counts, positions, here, *waits, adj_blocks, *rows)


def exchange(values, axes):
    return lax.all_to_all(values, axes, 0, 0)


def send_ahead(values, axes, distance):
    size = lax.axis_size(axes)
    return lax.ppermute(values, axes, [(i, (i + distance) % size) for i in range(size)])


def share(values, axes):
    copies = jnp.broadcast_to(values[None], (lax.axis_size(axes),) + values.shape)
    return exchange(lax.optimization_barrier(copies), axes)


def share_x(rows):
    return [rows] + [send_ahead(rows, "x", d) for d in range(1, lax.axis_size("x"))]


def pack(values, power):
    rows = values.shape[-2]
    padded = jnp.pad(values, [(0, 0)] * (values.ndim - 2) + [(0, 16), (0, 0)])
    row = lax.broadcasted_iota(jnp.int32, padded.shape, padded.ndim - 2)
    return jnp.where(row < rows, padded * jnp.exp2(14.0 - power), power).astype(jnp.float16)


def unpack(packed):
    power = packed[..., -1:, :1].astype(jnp.float32)
    return packed[..., :-16, :].astype(jnp.float32) / jnp.exp2(14.0 - power), jnp.max(power)


def local(features, adj_blocks, positions, counts, w_in, w_out, cotangent):
    slots, size = adj_blocks.shape[:2]
    nodes_dev, width = features.shape
    planes = lax.axis_size(("x", "y"))
    out_blocks = lax.axis_size(ROW) * nodes_dev // size
    in_blocks = lax.axis_size(COL) * nodes_dev // size
    spans = tuple(lax.axis_size(axis) for axis in COL)
    here = jnp.stack([lax.axis_index(axis) for axis in COL]).astype(jnp.int32)
    per_group = in_blocks // spans[0]

    def forward(groups, name, earlier=()):
        return tile_product(
            functools.partial(forward_kernel, spans),
            counts,
            positions,
            here,
            adj_blocks,
            groups,
            [(out_blocks, size, width)],
            name,
            earlier,
        )[0]

    near_one = share(features, ("y", "zl"))
    groups_one = share_x(near_one.reshape(per_group, size, width))
    group_grad = lax.all_gather(after(cotangent, near_one), "core", axis=0)
    group_grad = lax.all_gather(group_grad, "zh", axis=0).reshape(out_blocks, size, -1)
    *partial_two, top = tile_product(
        functools.partial(backward_kernel, spans),
        counts,
        positions,
        here,
        adj_blocks,
        [group_grad],
        [(per_group, size, width)] * spans[0] + [(8, size)],
        "backward",
        groups_one[1:],
    )
    bound = 0.01953125 * out_blocks * size
    most = jnp.clip(jnp.max(top), 1e-30, 1e38 / bound) * bound
    power = jnp.ceil(jnp.log2(most)) + 1.0
    flat = [part.reshape(-1, width) for part in partial_two]
    packed = lax.optimization_barrier([pack(part, power) for part in flat[1:]])

    partial_one = forward(groups_one, "forward_one", [packed[0][:16].astype(jnp.float32)])
    sums_one = exchange(partial_one, ROW)
    s_one = jnp.sum(sums_one, axis=0).astype(jnp.bfloat16)
    hidden = jnp.maximum(jnp.dot(s_one, w_in, preferred_element_type=jnp.float32), 0.0).astype(
        jnp.bfloat16
    )
    class_rows = jnp.dot(hidden, w_out, preferred_element_type=jnp.float32).astype(jnp.bfloat16)

    total = flat[0]
    for d, part in enumerate(packed, 1):
        part, other = unpack(send_ahead(part, "x", d))
        total, power = total + part, jnp.maximum(power, other)
    packed = pack(total.reshape(per_group, size, width), power + 2.0)
    sums_two = jnp.sum(unpack(exchange(packed, ("y", "zl")))[0], axis=0)
    d_two = sums_two.astype(jnp.bfloat16)

    near_two = share(after(class_rows, d_two), ("y", "zl"))
    groups_two = share_x(near_two.reshape(per_group, size, width))
    partial_out = forward(groups_two, "forward_two")

    local_out = jnp.einsum("nh,nc->hc", hidden, d_two, preferred_element_type=jnp.float32)
    d_hidden = jnp.einsum("nc,hc->nh", d_two, w_out, preferred_element_type=jnp.float32)
    masked = jnp.where(hidden > 0, d_hidden, 0.0).astype(jnp.bfloat16)
    local_in = jnp.einsum("nf,nh->fh", s_one, masked, preferred_element_type=jnp.float32)

    classes = local_out.shape[1]
    halves = local_in.shape[1] // classes
    parts = [local_in[:, i * classes : (i + 1) * classes] for i in range(halves)]
    grads = jnp.concatenate(parts + [local_out], axis=0).reshape(planes, -1, classes)
    grads = jnp.sum(exchange(grads, ("x", "y")), axis=0)
    output = jnp.sum(exchange(partial_out, ROW), axis=0).astype(jnp.bfloat16)
    for axis in ("zl", "core"):
        grads = jnp.sum(lax.all_gather(grads, axis, axis=0), axis=0)
    grads = jnp.sum(lax.all_gather(after(grads, partial_out), "zh", axis=0), axis=0)
    grads = share(grads, ("x", "y")).reshape(-1, classes)
    rows_in = local_in.shape[0]
    grad_in = jnp.concatenate(
        [grads[i * rows_in : (i + 1) * rows_in] for i in range(halves)], axis=1
    )
    grad_out = grads[halves * rows_in :]
    return (output, grad_in, grad_out)


def build(mesh, split):
    cut = Mesh(mesh.devices.reshape(tuple(split.values())), tuple(split))
    placed = (
        P(ALL, None),
        P(ALL, None, None),
        P(ALL, None),
        P(ALL),
        P(),
        P(),
        P(ALL, None),
    )
    return jax.shard_map(
        local,
        mesh=cut,
        in_specs=placed,
        out_specs=(P(ALL, None), P(), P()),
        check_vma=False,
    )


def solution(mesh):
    return build(mesh, SPLIT)
```

```python
import functools

import jax
import jax.numpy as jnp
from jax import lax
from jax.experimental import pallas as pl
from jax.experimental.pallas import tpu as pltpu
from jax.sharding import Mesh
from jax.sharding import PartitionSpec as P

SPLIT = {"zh": 4, "core": 2, "x": 4, "y": 8, "zl": 3}
ROW = ("zh", "core")
COL = ("x", "y", "zl")
ALL = ROW + COL
VMEM_LIMIT = 40 * 1024 * 1024


def ahead_of(place, here, size):
    return lax.rem(place - here + size, size)


def forward_kernel(spans, count_ref, place_ref, here_ref, blocks_ref, *refs):
    rows_refs, sums_ref = refs[:-1], refs[-1]
    per_group = rows_refs[0].shape[0]
    in_blocks = per_group * len(rows_refs)
    sums_ref[...] = jnp.zeros_like(sums_ref)

    def step(slot, carry):
        place = place_ref[0, slot]
        out_block = place // in_blocks
        in_block = place - out_block * in_blocks
        plane = in_block // per_group
        at = in_block - plane * per_group
        back_x = ahead_of(here_ref[0], plane, spans[0])
        for distance, rows_ref in enumerate(rows_refs):

            @pl.when(back_x == distance)
            def add(rows_ref=rows_ref):
                sums_ref[out_block] += jnp.dot(
                    blocks_ref[slot], rows_ref[at], preferred_element_type=jnp.float32
                )

        return carry

    lax.fori_loop(0, count_ref[0], step, 0)


def backward_kernel(spans, count_ref, place_ref, here_ref, blocks_ref, rows_ref, *refs):
    sums_refs, top_ref = refs[:-1], refs[-1]
    in_blocks = spans[0] * spans[1] * spans[2]
    for sums_ref in sums_refs:
        sums_ref[...] = jnp.zeros_like(sums_ref)

    def step(slot, top):
        place = place_ref[0, slot]
        out_block = place // in_blocks
        in_block = place - out_block * in_blocks
        line = in_block // spans[2]
        plane = line // spans[1]
        ahead_x = ahead_of(plane, here_ref[0], spans[0])
        at = in_block - plane * spans[1] * spans[2]
        block = blocks_ref[slot]
        product = lax.dot_general(
            block,
            rows_ref[out_block],
            (((0,), (0,)), ((), ())),
            preferred_element_type=jnp.float32,
        )
        for distance, sums_ref in enumerate(sums_refs):

            @pl.when(ahead_x == distance)
            def add(sums_ref=sums_ref):
                sums_ref[at] += product

        wide = block.astype(jnp.float32).reshape(-1, top.shape[0], top.shape[1])
        return jnp.maximum(top, jnp.max(wide, axis=0))

    top_ref[...] = lax.fori_loop(
        0, count_ref[0], step, jnp.zeros(top_ref.shape, jnp.float32)
    )


def after_kernel(values_ref, earlier_ref, out_ref):
    out_ref[...] = values_ref[...]


def after(values, earlier):
    return pl.pallas_call(
        after_kernel,
        out_shape=jax.ShapeDtypeStruct(values.shape, values.dtype),
        in_specs=[pl.BlockSpec(memory_space=pltpu.VMEM), pl.BlockSpec(memory_space=pl.ANY)],
        out_specs=pl.BlockSpec(memory_space=pltpu.VMEM),
        cost_estimate=pl.CostEstimate(flops=1, bytes_accessed=1, transcendentals=0),
        name="after",
    )(values, earlier)


def tile_product(kernel, counts, positions, here, adj_blocks, rows, outs, name, earlier=()):
    smem = pl.BlockSpec(memory_space=pltpu.SMEM)
    vmem = pl.BlockSpec(memory_space=pltpu.VMEM)
    outs = [jax.ShapeDtypeStruct(shape, jnp.float32) for shape in outs]
    waits = list(earlier)

    def body(count_ref, place_ref, here_ref, *refs):
        kernel(count_ref, place_ref, here_ref, *refs[len(waits) :])

    return pl.pallas_call(
        body,
        out_shape=outs,
        in_specs=[smem] * 3
        + [pl.BlockSpec(memory_space=pl.ANY)] * len(waits)
        + [vmem] * (1 + len(rows)),
        out_specs=[vmem] * len(outs),
        compiler_params=pltpu.CompilerParams(vmem_limit_bytes=VMEM_LIMIT),
        cost_estimate=pl.CostEstimate(flops=1, bytes_accessed=1, transcendentals=0),
        name=name,
    )(counts, positions, here, *waits, adj_blocks, *rows)


def exchange(values, axes):
    return lax.all_to_all(values, axes, 0, 0)


def send_ahead(values, axes, distance):
    size = lax.axis_size(axes)
    return lax.ppermute(values, axes, [(i, (i + distance) % size) for i in range(size)])


def share(values, axes):
    copies = jnp.broadcast_to(values[None], (lax.axis_size(axes),) + values.shape)
    return exchange(lax.optimization_barrier(copies), axes)


def share_x(rows):
    return [rows] + [send_ahead(rows, "x", d) for d in range(1, lax.axis_size("x"))]


def pack(values, power):
    rows = values.shape[-2]
    padded = jnp.pad(values, [(0, 0)] * (values.ndim - 2) + [(0, 16), (0, 0)])
    row = lax.broadcasted_iota(jnp.int32, padded.shape, padded.ndim - 2)
    return jnp.where(row < rows, padded * jnp.exp2(14.0 - power), power).astype(jnp.float16)


def unpack(packed, base=14.0):
    power = packed[..., -1:, :1].astype(jnp.float32)
    return packed[..., :-16, :].astype(jnp.float32) / jnp.exp2(base - power), jnp.max(power)


def local(features, adj_blocks, positions, counts, w_in, w_out, cotangent):
    slots, size = adj_blocks.shape[:2]
    nodes_dev, width = features.shape
    planes = lax.axis_size(("x", "y"))
    out_blocks = lax.axis_size(ROW) * nodes_dev // size
    in_blocks = lax.axis_size(COL) * nodes_dev // size
    spans = tuple(lax.axis_size(axis) for axis in COL)
    here = jnp.stack([lax.axis_index(axis) for axis in COL]).astype(jnp.int32)
    per_group = in_blocks // spans[0]

    def forward(groups, name, earlier=()):
        return tile_product(
            functools.partial(forward_kernel, spans),
            counts,
            positions,
            here,
            adj_blocks,
            groups,
            [(out_blocks, size, width)],
            name,
            earlier,
        )[0]

    near_one = share(features, ("y", "zl"))
    groups_one = share_x(near_one.reshape(per_group, size, width))
    group_grad = lax.all_gather(after(cotangent, near_one), "core", axis=0)
    group_grad = lax.all_gather(group_grad, "zh", axis=0).reshape(out_blocks, size, -1)
    *partial_two, top = tile_product(
        functools.partial(backward_kernel, spans),
        counts,
        positions,
        here,
        adj_blocks,
        [group_grad],
        [(per_group, size, width)] * spans[0] + [(8, size)],
        "backward",
    )
    partial_one = forward(groups_one, "forward_one", [group_grad])
    sums_one = exchange(partial_one, ROW)
    s_one = jnp.sum(sums_one, axis=0).astype(jnp.bfloat16)
    hidden = jnp.maximum(jnp.dot(s_one, w_in, preferred_element_type=jnp.float32), 0.0).astype(
        jnp.bfloat16
    )
    class_rows = jnp.dot(hidden, w_out, preferred_element_type=jnp.float32).astype(jnp.bfloat16)

    top = after(top, class_rows)
    bound = 0.01953125 * out_blocks * size
    most = jnp.clip(jnp.max(top), 1e-30, 1e38 / bound) * bound
    power = jnp.ceil(jnp.log2(most)) + 1.0
    flat = [part.reshape(-1, width) for part in partial_two]
    packed = lax.optimization_barrier([pack(part, power) for part in flat[1:]])

    near_two = lax.all_gather(lax.all_gather(class_rows, "zl", axis=0), "y", axis=0)
    groups_two = share_x(near_two.reshape(per_group, size, width))
    partial_out = forward(groups_two, "forward_two")

    base = after(jnp.full(top.shape, 14.0, jnp.float32), near_two)[0, 0]
    total = flat[0]
    for d, part in enumerate(packed, 1):
        part, other = unpack(send_ahead(part, "x", d), base)
        total, power = total + part, jnp.maximum(power, other)
    packed = pack(total.reshape(per_group, size, width), power + 2.0)
    sums_two = jnp.sum(unpack(exchange(packed, ("y", "zl")))[0], axis=0)
    d_two = sums_two.astype(jnp.bfloat16)

    local_out = jnp.einsum("nh,nc->hc", hidden, d_two, preferred_element_type=jnp.float32)
    d_hidden = jnp.einsum("nc,hc->nh", d_two, w_out, preferred_element_type=jnp.float32)
    masked = jnp.where(hidden > 0, d_hidden, 0.0).astype(jnp.bfloat16)
    local_in = jnp.einsum("nf,nh->fh", s_one, masked, preferred_element_type=jnp.float32)

    classes = local_out.shape[1]
    halves = local_in.shape[1] // classes
    parts = [local_in[:, i * classes : (i + 1) * classes] for i in range(halves)]
    grads = jnp.concatenate(parts + [local_out], axis=0).reshape(planes, -1, classes)
    grads = jnp.sum(exchange(grads, ("x", "y")), axis=0)
    output = jnp.sum(exchange(partial_out, ROW), axis=0).astype(jnp.bfloat16)
    grads = jnp.sum(share(after(grads, partial_out), ("zh", "core", "zl")), axis=0)
    grads = share(grads, ("x", "y")).reshape(-1, classes)
    rows_in = local_in.shape[0]
    grad_in = jnp.concatenate(
        [grads[i * rows_in : (i + 1) * rows_in] for i in range(halves)], axis=1
    )
    grad_out = grads[halves * rows_in :]
    return (output, grad_in, grad_out)


def build(mesh, split):
    cut = Mesh(mesh.devices.reshape(tuple(split.values())), tuple(split))
    placed = (
        P(ALL, None),
        P(ALL, None, None),
        P(ALL, None),
        P(ALL),
        P(),
        P(),
        P(ALL, None),
    )
    return jax.shard_map(
        local,
        mesh=cut,
        in_specs=placed,
        out_specs=(P(ALL, None), P(), P()),
        check_vma=False,
    )


def solution(mesh):
    return build(mesh, SPLIT)
```

```python
import functools

import jax
import jax.numpy as jnp
from jax import lax
from jax.experimental import pallas as pl
from jax.experimental.pallas import tpu as pltpu
from jax.sharding import Mesh
from jax.sharding import PartitionSpec as P

SPLIT = {"zh": 4, "core": 2, "x": 4, "y": 8, "zl": 3}
ROW = ("zh", "core")
COL = ("x", "y", "zl")
ALL = ROW + COL
VMEM_LIMIT = 40 * 1024 * 1024


def ahead_of(place, here, size):
    return lax.rem(place - here + size, size)


def forward_kernel(spans, count_ref, place_ref, here_ref, blocks_ref, *refs):
    rows_refs, sums_ref = refs[:-1], refs[-1]
    per_group = rows_refs[0].shape[0]
    in_blocks = per_group * len(rows_refs)
    sums_ref[...] = jnp.zeros_like(sums_ref)

    def step(slot, carry):
        place = place_ref[0, slot]
        out_block = place // in_blocks
        in_block = place - out_block * in_blocks
        plane = in_block // per_group
        at = in_block - plane * per_group
        back_x = ahead_of(here_ref[0], plane, spans[0])
        for distance, rows_ref in enumerate(rows_refs):

            @pl.when(back_x == distance)
            def add(rows_ref=rows_ref):
                sums_ref[out_block] += jnp.dot(
                    blocks_ref[slot], rows_ref[at], preferred_element_type=jnp.float32
                )

        return carry

    lax.fori_loop(0, count_ref[0], step, 0)


def backward_kernel(spans, count_ref, place_ref, here_ref, blocks_ref, rows_ref, *refs):
    sums_refs, top_ref = refs[:-1], refs[-1]
    in_blocks = spans[0] * spans[1] * spans[2]
    for sums_ref in sums_refs:
        sums_ref[...] = jnp.zeros_like(sums_ref)

    def step(slot, top):
        place = place_ref[0, slot]
        out_block = place // in_blocks
        in_block = place - out_block * in_blocks
        line = in_block // spans[2]
        plane = line // spans[1]
        ahead_x = ahead_of(plane, here_ref[0], spans[0])
        at = in_block - plane * spans[1] * spans[2]
        block = blocks_ref[slot]
        product = lax.dot_general(
            block,
            rows_ref[out_block],
            (((0,), (0,)), ((), ())),
            preferred_element_type=jnp.float32,
        )
        for distance, sums_ref in enumerate(sums_refs):

            @pl.when(ahead_x == distance)
            def add(sums_ref=sums_ref):
                sums_ref[at] += product

        wide = block.astype(jnp.float32).reshape(-1, top.shape[0], top.shape[1])
        return jnp.maximum(top, jnp.max(wide, axis=0))

    top_ref[...] = lax.fori_loop(
        0, count_ref[0], step, jnp.zeros(top_ref.shape, jnp.float32)
    )


def after_kernel(values_ref, earlier_ref, out_ref):
    out_ref[...] = values_ref[...]


def after(values, earlier):
    return pl.pallas_call(
        after_kernel,
        out_shape=jax.ShapeDtypeStruct(values.shape, values.dtype),
        in_specs=[pl.BlockSpec(memory_space=pltpu.VMEM), pl.BlockSpec(memory_space=pl.ANY)],
        out_specs=pl.BlockSpec(memory_space=pltpu.VMEM),
        cost_estimate=pl.CostEstimate(flops=1, bytes_accessed=1, transcendentals=0),
        name="after",
    )(values, earlier)


def tile_product(kernel, counts, positions, here, adj_blocks, rows, outs, name, earlier=()):
    smem = pl.BlockSpec(memory_space=pltpu.SMEM)
    vmem = pl.BlockSpec(memory_space=pltpu.VMEM)
    outs = [jax.ShapeDtypeStruct(shape, jnp.float32) for shape in outs]
    waits = list(earlier)

    def body(count_ref, place_ref, here_ref, *refs):
        kernel(count_ref, place_ref, here_ref, *refs[len(waits) :])

    return pl.pallas_call(
        body,
        out_shape=outs,
        in_specs=[smem] * 3
        + [pl.BlockSpec(memory_space=pl.ANY)] * len(waits)
        + [vmem] * (1 + len(rows)),
        out_specs=[vmem] * len(outs),
        compiler_params=pltpu.CompilerParams(vmem_limit_bytes=VMEM_LIMIT),
        cost_estimate=pl.CostEstimate(flops=1, bytes_accessed=1, transcendentals=0),
        name=name,
    )(counts, positions, here, *waits, adj_blocks, *rows)


def exchange(values, axes):
    return lax.all_to_all(values, axes, 0, 0)


def send_ahead(values, axes, distance):
    size = lax.axis_size(axes)
    return lax.ppermute(values, axes, [(i, (i + distance) % size) for i in range(size)])


def share(values, axes):
    copies = jnp.broadcast_to(values[None], (lax.axis_size(axes),) + values.shape)
    return exchange(lax.optimization_barrier(copies), axes)


def share_x(rows):
    return [rows] + [send_ahead(rows, "x", d) for d in range(1, lax.axis_size("x"))]


def pack(values, power):
    rows = values.shape[-2]
    padded = jnp.pad(values, [(0, 0)] * (values.ndim - 2) + [(0, 16), (0, 0)])
    row = lax.broadcasted_iota(jnp.int32, padded.shape, padded.ndim - 2)
    return jnp.where(row < rows, padded * jnp.exp2(14.0 - power), power).astype(jnp.float16)


def unpack(packed, base=14.0):
    power = packed[..., -1:, :].astype(jnp.float32)
    return packed[..., :-16, :].astype(jnp.float32) / jnp.exp2(base - power), power


def local(features, adj_blocks, positions, counts, w_in, w_out, cotangent):
    slots, size = adj_blocks.shape[:2]
    nodes_dev, width = features.shape
    planes = lax.axis_size(("x", "y"))
    out_blocks = lax.axis_size(ROW) * nodes_dev // size
    in_blocks = lax.axis_size(COL) * nodes_dev // size
    spans = tuple(lax.axis_size(axis) for axis in COL)
    here = jnp.stack([lax.axis_index(axis) for axis in COL]).astype(jnp.int32)
    per_group = in_blocks // spans[0]

    def forward(groups, name, earlier=()):
        return tile_product(
            functools.partial(forward_kernel, spans),
            counts,
            positions,
            here,
            adj_blocks,
            groups,
            [(out_blocks, size, width)],
            name,
            earlier,
        )[0]

    near_one = share(features, ("y", "zl"))
    groups_one = share_x(near_one.reshape(per_group, size, width))
    group_grad = lax.all_gather(after(cotangent, near_one), "core", axis=0)
    group_grad = lax.all_gather(group_grad, "zh", axis=0).reshape(out_blocks, size, -1)
    *partial_two, top = tile_product(
        functools.partial(backward_kernel, spans),
        counts,
        positions,
        here,
        adj_blocks,
        [group_grad],
        [(per_group, size, width)] * spans[0] + [(8, size)],
        "backward",
    )
    partial_one = forward(groups_one, "forward_one", [group_grad])
    sums_one = exchange(partial_one, ROW)
    s_one = jnp.sum(sums_one, axis=0).astype(jnp.bfloat16)
    hidden = jnp.maximum(jnp.dot(s_one, w_in, preferred_element_type=jnp.float32), 0.0).astype(
        jnp.bfloat16
    )
    class_rows = jnp.dot(hidden, w_out, preferred_element_type=jnp.float32).astype(jnp.bfloat16)

    bound = 0.01953125 * out_blocks * size
    most = jnp.clip(jnp.max(top), 1e-30, 1e38 / bound) * bound
    power = jnp.broadcast_to(jnp.ceil(jnp.log2(most)) + 1.0, top.shape)
    power = after(power, class_rows)[:1]
    flat = [part.reshape(-1, width) for part in partial_two]
    packed = lax.optimization_barrier([pack(part, power) for part in flat[1:]])

    near_two = lax.all_gather(lax.all_gather(class_rows, "zl", axis=0), "y", axis=0)
    groups_two = share_x(near_two.reshape(per_group, size, width))
    partial_out = forward(groups_two, "forward_two")

    base = after(jnp.full(top.shape, 14.0, jnp.float32), near_two)[:1]
    total = flat[0]
    for d, part in enumerate(packed, 1):
        part, other = unpack(send_ahead(part, "x", d), base)
        total, power = total + part, jnp.maximum(power, other)
    packed = pack(total.reshape(per_group, size, width), power + 2.0)
    sums_two = jnp.sum(unpack(exchange(packed, ("y", "zl")))[0], axis=0)
    d_two = sums_two.astype(jnp.bfloat16)

    local_out = jnp.einsum("nh,nc->hc", hidden, d_two, preferred_element_type=jnp.float32)
    d_hidden = jnp.einsum("nc,hc->nh", d_two, w_out, preferred_element_type=jnp.float32)
    masked = jnp.where(hidden > 0, d_hidden, 0.0).astype(jnp.bfloat16)
    local_in = jnp.einsum("nf,nh->fh", s_one, masked, preferred_element_type=jnp.float32)

    classes = local_out.shape[1]
    halves = local_in.shape[1] // classes
    parts = [local_in[:, i * classes : (i + 1) * classes] for i in range(halves)]
    grads = jnp.concatenate(parts + [local_out], axis=0).reshape(planes, -1, classes)
    grads = jnp.sum(exchange(grads, ("x", "y")), axis=0)
    output = jnp.sum(exchange(partial_out, ROW), axis=0).astype(jnp.bfloat16)
    grads = jnp.sum(share(after(grads, partial_out), ("zh", "core", "zl")), axis=0)
    grads = share(grads, ("x", "y")).reshape(-1, classes)
    rows_in = local_in.shape[0]
    grad_in = jnp.concatenate(
        [grads[i * rows_in : (i + 1) * rows_in] for i in range(halves)], axis=1
    )
    grad_out = grads[halves * rows_in :]
    return (output, grad_in, grad_out)


def build(mesh, split):
    cut = Mesh(mesh.devices.reshape(tuple(split.values())), tuple(split))
    placed = (
        P(ALL, None),
        P(ALL, None, None),
        P(ALL, None),
        P(ALL),
        P(),
        P(),
        P(ALL, None),
    )
    return jax.shard_map(
        local,
        mesh=cut,
        in_specs=placed,
        out_specs=(P(ALL, None), P(), P()),
        check_vma=False,
    )


def solution(mesh):
    return build(mesh, SPLIT)
```

```python
import functools

import jax
import jax.numpy as jnp
from jax import lax
from jax.experimental import pallas as pl
from jax.experimental.pallas import tpu as pltpu
from jax.sharding import Mesh
from jax.sharding import PartitionSpec as P

SPLIT = {"zh": 4, "core": 2, "x": 4, "y": 8, "zl": 3}
ROW = ("zh", "core")
COL = ("x", "y", "zl")
ALL = ROW + COL
VMEM_LIMIT = 40 * 1024 * 1024


def ahead_of(place, here, size):
    return lax.rem(place - here + size, size)


def forward_kernel(spans, count_ref, place_ref, here_ref, blocks_ref, *refs):
    rows_refs, sums_ref = refs[:-1], refs[-1]
    per_group = rows_refs[0].shape[0]
    in_blocks = per_group * len(rows_refs)
    sums_ref[...] = jnp.zeros_like(sums_ref)

    def step(slot, carry):
        place = place_ref[0, slot]
        out_block = place // in_blocks
        in_block = place - out_block * in_blocks
        plane = in_block // per_group
        at = in_block - plane * per_group
        back_x = ahead_of(here_ref[0], plane, spans[0])
        for distance, rows_ref in enumerate(rows_refs):

            @pl.when(back_x == distance)
            def add(rows_ref=rows_ref):
                sums_ref[out_block] += jnp.dot(
                    blocks_ref[slot], rows_ref[at], preferred_element_type=jnp.float32
                )

        return carry

    lax.fori_loop(0, count_ref[0], step, 0)


def backward_kernel(spans, count_ref, place_ref, here_ref, blocks_ref, rows_ref, *refs):
    sums_refs, top_ref = refs[:-1], refs[-1]
    in_blocks = spans[0] * spans[1] * spans[2]
    for sums_ref in sums_refs:
        sums_ref[...] = jnp.zeros_like(sums_ref)

    def step(slot, top):
        place = place_ref[0, slot]
        out_block = place // in_blocks
        in_block = place - out_block * in_blocks
        line = in_block // spans[2]
        plane = line // spans[1]
        ahead_x = ahead_of(plane, here_ref[0], spans[0])
        at = in_block - plane * spans[1] * spans[2]
        block = blocks_ref[slot]
        product = lax.dot_general(
            block,
            rows_ref[out_block],
            (((0,), (0,)), ((), ())),
            preferred_element_type=jnp.float32,
        )
        for distance, sums_ref in enumerate(sums_refs):

            @pl.when(ahead_x == distance)
            def add(sums_ref=sums_ref):
                sums_ref[at] += product

        wide = block.astype(jnp.float32).reshape(-1, top.shape[0], top.shape[1])
        return jnp.maximum(top, jnp.max(wide, axis=0))

    top_ref[...] = lax.fori_loop(
        0, count_ref[0], step, jnp.zeros(top_ref.shape, jnp.float32)
    )


def after_kernel(values_ref, earlier_ref, out_ref):
    out_ref[...] = values_ref[...]


def after(values, earlier):
    return pl.pallas_call(
        after_kernel,
        out_shape=jax.ShapeDtypeStruct(values.shape, values.dtype),
        in_specs=[pl.BlockSpec(memory_space=pltpu.VMEM), pl.BlockSpec(memory_space=pl.ANY)],
        out_specs=pl.BlockSpec(memory_space=pltpu.VMEM),
        cost_estimate=pl.CostEstimate(flops=1, bytes_accessed=1, transcendentals=0),
        name="after",
    )(values, earlier)


def tile_product(kernel, counts, positions, here, adj_blocks, rows, outs, name, earlier=()):
    smem = pl.BlockSpec(memory_space=pltpu.SMEM)
    vmem = pl.BlockSpec(memory_space=pltpu.VMEM)
    outs = [jax.ShapeDtypeStruct(shape, jnp.float32) for shape in outs]
    waits = list(earlier)

    def body(count_ref, place_ref, here_ref, *refs):
        kernel(count_ref, place_ref, here_ref, *refs[len(waits) :])

    return pl.pallas_call(
        body,
        out_shape=outs,
        in_specs=[smem] * 3
        + [pl.BlockSpec(memory_space=pl.ANY)] * len(waits)
        + [vmem] * (1 + len(rows)),
        out_specs=[vmem] * len(outs),
        compiler_params=pltpu.CompilerParams(vmem_limit_bytes=VMEM_LIMIT),
        cost_estimate=pl.CostEstimate(flops=1, bytes_accessed=1, transcendentals=0),
        name=name,
    )(counts, positions, here, *waits, adj_blocks, *rows)


def exchange(values, axes):
    return lax.all_to_all(values, axes, 0, 0)


def send_ahead(values, axes, distance):
    size = lax.axis_size(axes)
    return lax.ppermute(values, axes, [(i, (i + distance) % size) for i in range(size)])


def share(values, axes):
    copies = jnp.broadcast_to(values[None], (lax.axis_size(axes),) + values.shape)
    return exchange(lax.optimization_barrier(copies), axes)


def share_x(rows):
    return [rows] + [send_ahead(rows, "x", d) for d in range(1, lax.axis_size("x"))]


def pack(values, power):
    rows = values.shape[-2]
    padded = jnp.pad(values, [(0, 0)] * (values.ndim - 2) + [(0, 16), (0, 0)])
    row = lax.broadcasted_iota(jnp.int32, padded.shape, padded.ndim - 2)
    return jnp.where(row < rows, padded * jnp.exp2(14.0 - power), power).astype(jnp.float16)


def unpack(packed, base=14.0):
    power = packed[..., -1:, :].astype(jnp.float32)
    return packed[..., :-16, :].astype(jnp.float32) / jnp.exp2(base - power), power


def local(features, adj_blocks, positions, counts, w_in, w_out, cotangent):
    slots, size = adj_blocks.shape[:2]
    nodes_dev, width = features.shape
    planes = lax.axis_size(("x", "y"))
    out_blocks = lax.axis_size(ROW) * nodes_dev // size
    in_blocks = lax.axis_size(COL) * nodes_dev // size
    spans = tuple(lax.axis_size(axis) for axis in COL)
    here = jnp.stack([lax.axis_index(axis) for axis in COL]).astype(jnp.int32)
    per_group = in_blocks // spans[0]

    def forward(groups, name, earlier=()):
        return tile_product(
            functools.partial(forward_kernel, spans),
            counts,
            positions,
            here,
            adj_blocks,
            groups,
            [(out_blocks, size, width)],
            name,
            earlier,
        )[0]

    near_one = share(features, ("y", "zl"))
    groups_one = share_x(near_one.reshape(per_group, size, width))
    group_grad = lax.all_gather(after(cotangent, near_one), "core", axis=0)
    group_grad = lax.all_gather(group_grad, "zh", axis=0).reshape(out_blocks, size, -1)
    *partial_two, top = tile_product(
        functools.partial(backward_kernel, spans),
        counts,
        positions,
        here,
        adj_blocks,
        [group_grad],
        [(per_group, size, width)] * spans[0] + [(8, size)],
        "backward",
    )
    partial_one = forward(groups_one, "forward_one", [group_grad])
    sums_one = exchange(partial_one, ROW)
    s_one = jnp.sum(sums_one, axis=0).astype(jnp.bfloat16)
    hidden = jnp.maximum(jnp.dot(s_one, w_in, preferred_element_type=jnp.float32), 0.0).astype(
        jnp.bfloat16
    )
    class_rows = jnp.dot(hidden, w_out, preferred_element_type=jnp.float32).astype(jnp.bfloat16)

    bound = 0.01953125 * out_blocks * size
    most = jnp.clip(jnp.max(top), 1e-30, 1e38 / bound) * bound
    power = jnp.broadcast_to(jnp.ceil(jnp.log2(most)) + 1.0, top.shape)
    power = after(power, class_rows)[:1]
    flat = [part.reshape(-1, width) for part in partial_two]
    packed = lax.optimization_barrier([pack(part, power) for part in flat[1:]])

    near_two = lax.all_gather(lax.all_gather(class_rows, "zl", axis=0), "y", axis=0)
    groups_two = share_x(near_two.reshape(per_group, size, width))
    partial_out = forward(groups_two, "forward_two")

    base = after(jnp.full(top.shape, 14.0, jnp.float32), near_two)[:1]
    total = flat[0]
    for d, part in enumerate(packed, 1):
        part, other = unpack(send_ahead(part, "x", d), base)
        total, power = total + part, jnp.maximum(power, other)
    packed = pack(total.reshape(per_group, size, width), power + 2.0)
    sums_two = jnp.sum(unpack(exchange(packed, ("y", "zl")))[0], axis=0)
    d_two = sums_two.astype(jnp.bfloat16)

    local_out = jnp.einsum("nh,nc->hc", hidden, d_two, preferred_element_type=jnp.float32)
    d_hidden = jnp.einsum("nc,hc->nh", d_two, w_out, preferred_element_type=jnp.float32)
    masked = jnp.where(hidden > 0, d_hidden, 0.0).astype(jnp.bfloat16)
    local_in = jnp.einsum("nf,nh->fh", s_one, masked, preferred_element_type=jnp.float32)

    classes = local_out.shape[1]
    halves = local_in.shape[1] // classes
    parts = [local_in[:, i * classes : (i + 1) * classes] for i in range(halves)]
    grads = jnp.concatenate(parts + [local_out], axis=0).reshape(planes, -1, classes)
    grads = jnp.sum(exchange(grads, ("x", "y")), axis=0)
    copies = jnp.broadcast_to(grads[None], (lax.axis_size(ROW),) + grads.shape)
    last = exchange(jnp.concatenate([partial_out, copies], axis=1), ROW)
    last = jnp.sum(last, axis=0)
    output = last[:size].astype(jnp.bfloat16)
    grads = jnp.sum(lax.all_gather(last[size:], "zl", axis=0), axis=0)
    grads = share(grads, ("x", "y")).reshape(-1, classes)
    rows_in = local_in.shape[0]
    grad_in = jnp.concatenate(
        [grads[i * rows_in : (i + 1) * rows_in] for i in range(halves)], axis=1
    )
    grad_out = grads[halves * rows_in :]
    return (output, grad_in, grad_out)


def build(mesh, split):
    cut = Mesh(mesh.devices.reshape(tuple(split.values())), tuple(split))
    placed = (
        P(ALL, None),
        P(ALL, None, None),
        P(ALL, None),
        P(ALL),
        P(),
        P(),
        P(ALL, None),
    )
    return jax.shard_map(
        local,
        mesh=cut,
        in_specs=placed,
        out_specs=(P(ALL, None), P(), P()),
        check_vma=False,
    )


def solution(mesh):
    return build(mesh, SPLIT)
```
